512 devices in a mesh: row: 32 (over y, x, core), col: 16 (over z).
Axes of the slice: x: 4, y: 4, z: 16, core: 2. Of those that a mesh axis runs over, the one named last changes fastest.
Arguments:
- inputs: float32 [262144, 128], P(('row', 'col')), may hold values from -6 to 6
- tasks: int32 [262144], P(('row', 'col')), may hold values from 0 to 7
- targets: float32 [262144], P(('row', 'col')), may hold values from -6 to 6
- inv_length: float32 [128], replicated, may hold values from 0.02 to 0.2
- task_factor: float32 [8, 8], replicated, may hold values from -2 to 2
- task_diag: float32 [8], replicated, may hold values from 0.3 to 1
- noise: float32 [8], replicated, may hold values from 0.05 to 0.5
- pivots: int32 [2, 64], replicated, may hold values from 0 to 262143, as said below
- test_inputs: float32 [16384, 128], P('row'), may hold values from -6 to 6
- test_tasks: int32 [16384], P('row'), may hold values from 0 to 7
Outputs:
- residual_diag: float32 [262144], P(('row', 'col'))
- lanczos_next: float32 [16384], P(('row', 'col'))
- test_coef: float32 [16384], P('row')
The draws below stay inside these ranges and needn't reach their ends.
Inputs may be any that keep to these rules, and one draw needn't show every extreme that they name: `pivots`: all 128 pivot indices are distinct.
All inputs are finite; a program needn't handle non-finite values.
Results may differ from the reference program's by a relative error of at most 0.0003.
Values sent between devices are 32-bit elements; how exact they have to be, the bound alone decides.
A program may use at most 64 MiB of HBM per device.

```python
import math
import jax
import jax.numpy as jnp
from jax import lax

DX = 128
TASKS = 8
PIV = 64
SUB = 32
N = 262144
TEST = 16384
N_ROW = 32
N_COL = 16


def draw_pivots(key, part):
    key = jax.random.fold_in(key, 7)
    order = jax.random.permutation(key, N)
    return order[:2 * PIV].reshape(2, PIV).astype(jnp.int32)


def set_ends(drawn, rng, smallest, high):
    longest = drawn.shape.index(max(drawn.shape))
    spots = []
    for shift in (0, 1):
        where = [jax.random.randint(jax.random.fold_in(rng, axis), (), 0, length) for axis, length in enumerate(drawn.shape)]
        where[longest] = (where[longest] + shift) % drawn.shape[longest]
        spots.append(tuple(where))
    return drawn.at[spots[0]].set(smallest).at[spots[1]].set(high)


def steps_of(rng, dims, shards, least, high):
    level, own = 1.0, jax.random.fold_in(rng, 6)
    for axis_at, parts in shards:
        steps = jnp.exp(jax.random.uniform(jax.random.fold_in(own, axis_at), (parts,), jnp.float32, least / len(shards), high / len(shards)))
        level = level * jnp.repeat(steps, dims[axis_at] // parts).reshape([-1 if axis == axis_at else 1 for axis in range(len(dims))])
    return level


def centred(key, shape, deviation, limit, shards=(), held_as=jnp.bfloat16):
    factor_of = steps_of(key, shape, shards, -0.22, 0.18) if shards else 1.0
    drawn = jax.random.normal(key, shape, jnp.float32) * deviation * factor_of
    return jnp.minimum(jnp.maximum(drawn, -limit), limit).astype(held_as)


def setup_inputs(seed: int = 0) -> dict:
    key_list = jax.random.split(jax.random.key(seed), 11)
    inputs = centred(key_list[0], (N, DX), 1.0, 6.0, ((0, 512),), jnp.float32)
    tasks = set_ends(jax.random.randint(key_list[1], (N,), 0, TASKS), jax.random.fold_in(key_list[1], 1), 0, TASKS - 1).astype(jnp.int32)
    targets = centred(key_list[2], (N,), 1.0, 6.0, ((0, 512),), jnp.float32)
    inv_length = jnp.clip(jnp.exp(jax.random.uniform(key_list[3], (DX,), jnp.float32, math.log(0.02), math.log(0.2))), 0.02, 0.2)
    task_factor = centred(key_list[4], (TASKS, TASKS), TASKS ** -0.5, 2.0, (), jnp.float32)
    task_diag = jnp.clip(jnp.exp(jax.random.uniform(key_list[5], (TASKS,), jnp.float32, math.log(0.3), math.log(1.0))), 0.3, 1.0)
    noise = jnp.clip(jnp.exp(jax.random.uniform(key_list[6], (TASKS,), jnp.float32, math.log(0.05), math.log(0.5))), 0.05, 0.5)
    pivots = draw_pivots(jax.random.fold_in(key_list[10], 71), 0)
    test_inputs = centred(key_list[8], (TEST, DX), 1.0, 6.0, ((0, 32),), jnp.float32)
    test_tasks = set_ends(jax.random.randint(key_list[9], (TEST,), 0, TASKS), jax.random.fold_in(key_list[9], 1), 0, TASKS - 1).astype(jnp.int32)
    return {"inputs": inputs, "tasks": tasks, "targets": targets, "inv_length": inv_length, "task_factor": task_factor, "task_diag": task_diag, "noise": noise, "pivots": pivots, "test_inputs": test_inputs, "test_tasks": test_tasks}


def right_solve(low, mat):
    return lax.linalg.triangular_solve(low, mat, left_side=False, lower=True, transpose_a=True)

def cho_apply(low, vec):
    column = vec[:, None]
    inner = lax.linalg.triangular_solve(low, column, left_side=True, lower=True)
    outer = lax.linalg.triangular_solve(low, inner, left_side=True, lower=True, transpose_a=True)
    return outer[:, 0]

def kernel_tile(a_rows, oh_rows, a_cols, oh_cols, task_cov):
    high = lax.Precision.HIGHEST
    sq_rows = lax.optimization_barrier(jnp.sum(a_rows * a_rows, axis=1))
    sq_cols = lax.optimization_barrier(jnp.sum(a_cols * a_cols, axis=1))
    cross = jnp.dot(a_rows, a_cols.T, precision=high)
    dist = sq_rows[:, None] + sq_cols[None, :] - 2.0 * cross
    scale = jnp.dot(jnp.dot(oh_rows, task_cov, precision=high), oh_cols.T, precision=high)
    return jnp.exp(-0.5 * dist) * scale

def reference(inputs, tasks, targets, inv_length, task_factor, task_diag, noise, pivots, test_inputs, test_tasks):
    high = lax.Precision.HIGHEST
    task_cov = jnp.dot(task_factor, task_factor.T, precision=high) + jnp.diag(task_diag)
    scaled = inputs * inv_length[None, :]
    onehot = jax.nn.one_hot(tasks, TASKS, dtype=jnp.float32)
    first_piv = pivots[0]
    second_piv = pivots[1]
    a_one = scaled[first_piv]
    oh_one = onehot[first_piv]
    a_two = scaled[second_piv]
    oh_two = onehot[second_piv]
    lower_one = jnp.linalg.cholesky(kernel_tile(a_one, oh_one, a_one, oh_one, task_cov))
    cols_one = kernel_tile(scaled, onehot, a_one, oh_one, task_cov)
    first = right_solve(lower_one, cols_one)
    first_two = first[second_piv]
    schur = kernel_tile(a_two, oh_two, a_two, oh_two, task_cov) - jnp.dot(first_two, first_two.T, precision=high)
    lower_two = jnp.linalg.cholesky(schur)
    cols_two = kernel_tile(scaled, onehot, a_two, oh_two, task_cov) - jnp.dot(first, first_two.T, precision=high)
    second = right_solve(lower_two, cols_two)
    bdiag = jnp.dot(onehot, jnp.diag(task_cov), precision=high)
    residual_diag = bdiag - lax.optimization_barrier(jnp.sum(first * first, axis=1)) - lax.optimization_barrier(jnp.sum(second * second, axis=1))
    devices = N_ROW * N_COL
    rows_dev = inputs.shape[0] // devices
    factor = jnp.concatenate([first, second], axis=1)

    def slab_of(arr):
        shaped = arr.reshape((devices, rows_dev) + arr.shape[1:])
        return shaped[:, :SUB].reshape((devices * SUB,) + arr.shape[1:])
    a_slab = slab_of(scaled)
    oh_slab = slab_of(onehot)
    factor_s = slab_of(factor)
    y_slab = slab_of(targets)
    dvec = jnp.dot(oh_slab, noise, precision=high)
    inv_d = 1.0 / dvec
    gram = jnp.dot(factor_s.T, inv_d[:, None] * factor_s, precision=high)
    proj = jnp.dot(factor_s.T, y_slab * inv_d, precision=high)
    yy = jnp.sum(y_slab * y_slab * inv_d)
    cap = jnp.eye(2 * PIV, dtype=jnp.float32) + gram
    cap_low = jnp.linalg.cholesky(cap)
    cap_proj = cho_apply(cap_low, proj)
    zvec = (y_slab - jnp.dot(factor_s, cap_proj, precision=high)) * inv_d
    gamma = yy - jnp.sum(proj * cap_proj)
    qvec = zvec / jnp.sqrt(gamma)
    slab_len = a_slab.shape[0]
    block = math.gcd(slab_len, 512)

    def slab_block(idx):
        ra = lax.dynamic_slice_in_dim(a_slab, idx * block, block, 0)
        roh = lax.dynamic_slice_in_dim(oh_slab, idx * block, block, 0)
        return jnp.dot(kernel_tile(ra, roh, a_slab, oh_slab, task_cov), qvec, precision=high)
    kprod = lax.map(slab_block, jnp.arange(slab_len // block)).reshape(slab_len)
    wvec = kprod + dvec * qvec
    alpha = jnp.sum(qvec * wvec)
    back = jnp.dot(factor_s.T, wvec * inv_d, precision=high)
    lanczos_next = (wvec - jnp.dot(factor_s, cho_apply(cap_low, back), precision=high)) * inv_d - alpha * qvec
    test_a = test_inputs * inv_length[None, :]
    test_oh = jax.nn.one_hot(test_tasks, TASKS, dtype=jnp.float32)
    test_len = test_a.shape[0]
    tblock = math.gcd(test_len, 512)

    def test_block(idx):
        ra = lax.dynamic_slice_in_dim(test_a, idx * tblock, tblock, 0)
        roh = lax.dynamic_slice_in_dim(test_oh, idx * tblock, tblock, 0)
        return jnp.dot(kernel_tile(ra, roh, a_slab, oh_slab, task_cov), qvec, precision=high)
    kq = lax.map(test_block, jnp.arange(test_len // tblock)).reshape(test_len)
    test_coef = kq / jnp.sqrt(alpha)
    return (residual_diag, lanczos_next, test_coef)
```

```python
import functools

import jax
import jax.numpy as jnp
from jax import lax
from jax.experimental import pallas as pl
from jax.experimental.pallas import tpu as pltpu
from jax.sharding import PartitionSpec as P

TASKS = 8
PIV = 64
NP = 2 * PIV
SUB = 32
LANES = 128
HIGH = lax.Precision.HIGHEST
MESH = pl.DeviceIdType.MESH
F32 = jnp.float32

RS1, Z1, AG1, SLC, SLR, Z2, AG2, Z3, P3 = range(9)


def iota(shape, axis):
    return lax.broadcasted_iota(jnp.int32, shape, axis)


def mm(a, b, precision=HIGH):
    return lax.dot_general(a, b, (((1,), (0,)), ((), ())), precision=precision, preferred_element_type=F32)


def mm_nt(a, b, precision=HIGH):
    return lax.dot_general(a, b, (((1,), (1,)), ((), ())), precision=precision, preferred_element_type=F32)


def diag_to_row(col, eye):
    return jnp.sum(jnp.where(eye, col, 0.0), axis=0, keepdims=True)


def row_to_col(row, eye):
    return jnp.sum(jnp.where(eye, row, 0.0), axis=1, keepdims=True)


def onehot_rows(task_row):
    n = task_row.shape[1]
    return (iota((TASKS, n), 0).astype(F32) == task_row).astype(F32)


def half_sq_row(a):
    ones = jnp.full((8, a.shape[1]), 0.5, F32)
    return mm_nt(ones, a * a)[0:1, :]


def eliminate(a, lane):
    top = a[0:8, :]
    cols = [jnp.broadcast_to(top[:, m : m + 1], (8, LANES)) for m in range(8)]
    d = [[cols[m][i : i + 1, :] for m in range(8)] for i in range(8)]
    rows = [jnp.where(lane < 8, (lane == i).astype(F32), top[i : i + 1, :]) for i in range(8)]
    for m in range(8):
        inv = 1.0 / d[m][m]
        rows[m] = rows[m] * inv
        for j in range(m + 1, 8):
            d[m][j] = d[m][j] * inv
        for i in range(8):
            if i != m:
                f = d[i][m]
                rows[i] = rows[i] - f * rows[m]
                for j in range(m + 1, 8):
                    d[i][j] = d[i][j] - f * d[m][j]
    body = a[8:, :]
    acc = jnp.where(lane < 8, 0.0, body)
    for m in range(8):
        acc = acc - body[:, m : m + 1] * rows[m]
    out = jnp.concatenate([acc] + rows, axis=0)
    return pltpu.roll(out, LANES - 8, axis=1)


def kernel(
    nr, nc,
    pivots, tasks_s, inputs, tasks, targets, il, tfac, tdiag, noise, tests, ttasks,
    res_o, ln_o, tc_o,
    psrc, rsbuf, zsrc1, zbuf1, apiv, agsrc1, slsrc, bufc, bufr,
    zsrc2, zbuf2, agsrc2, gram, zsrc3, zbuf3, psrc3, pbuf3,
    art, kmat, gt_c, gt_r, kp_own, mmat, pmat,
    ssem, rsem,
):
    r = lax.axis_index("row")
    c = lax.axis_index("col")
    me = r * nc + c
    chunks = nr // 2
    cr = NP // chunks
    mine = r // 2
    rows_dev = inputs.shape[0]
    nown = rows_dev // LANES
    ntest = tests.shape[0] // LANES
    nrr = nc * SUB
    ncc = nr * SUB
    prr, pcc = nrr // LANES, ncc // LANES

    def in_row(k):
        return lax.rem(r + k, nr)

    def in_col(k):
        return lax.rem(c + k, nc)

    order_z = sorted(range(1, nc), key=lambda k: -min(k, nc - k))
    order_p = list(range(1, nr))

    bar = pltpu.get_barrier_semaphore()
    for k in order_z:
        pl.semaphore_signal(bar, inc=1, device_id={"row": r, "col": in_col(k)}, device_id_type=MESH)
    for k in order_p:
        pl.semaphore_signal(bar, inc=1, device_id={"row": in_row(k), "col": c}, device_id_type=MESH)

    def send_z(src, dst, sem):
        for k in order_z:
            pltpu.make_async_remote_copy(
                src, dst, ssem.at[sem], rsem.at[sem], device_id={"row": r, "col": in_col(k)}, device_id_type=MESH
            ).start()

    def send_p(src_of, dst, sem, step=1):
        for k in order_p:
            if k % step == 0:
                to = in_row(k)
                pltpu.make_async_remote_copy(
                    src_of(to), dst, ssem.at[sem], rsem.at[sem], device_id={"row": to, "col": c}, device_id_type=MESH
                ).start()

    def wait(ref, sem):
        pltpu.make_async_copy(ref, ref, sem).wait()

    lane = iota((1, LANES), 1)
    eye8 = iota((TASKS, TASKS), 0) == iota((TASKS, TASKS), 1)
    eye = iota((NP, NP), 0) == iota((NP, NP), 1)
    scale = il[...]
    cov = mm_nt(tfac[...], tfac[...]) + jnp.where(eye8, jnp.broadcast_to(tdiag[...], (TASKS, TASKS)), 0.0)
    noise_col = row_to_col(jnp.broadcast_to(noise[...], (TASKS, TASKS)), eye8)

    def pick(i, trow):
        piv = pivots[i // PIV, lax.rem(i, PIV)]
        own = (piv // rows_dev == me).astype(F32)
        loc = lax.rem(piv, rows_dev)
        row = inputs[pl.ds(loc, 1), :] * scale * own
        psrc[i // cr, pl.ds(lax.rem(i, cr), 1), :] = row
        return trow + jnp.where(lane == i, tasks_s[loc].astype(F32) * own, 0.0)

    trow = lax.fori_loop(0, NP, pick, jnp.zeros((1, LANES), F32))
    for j in range(chunks):
        psrc[j, cr : cr + 1, :] = trow

    slsrc[0:SUB, :] = inputs[0:SUB, :] * scale
    t_own = tasks[0:1, 0:SUB].astype(F32)
    y_own = targets[0:1, 0:SUB]
    t4 = jnp.concatenate([t_own] * 4, axis=1)
    y4 = jnp.concatenate([y_own] * 4, axis=1)
    at_r = lane // SUB == lax.rem(r, 4)
    at_c = lane // SUB == lax.rem(c, 4)
    slsrc[SUB : SUB + 1, :] = jnp.where(at_r, t4, 0.0)
    slsrc[SUB + 1 : SUB + 2, :] = jnp.where(at_r, y4, 0.0)
    slsrc[SUB + 2 : SUB + 3, :] = jnp.where(at_c, t4, 0.0)
    slsrc[SUB + 3 : SUB + 4, :] = jnp.where(at_c, y4, 0.0)
    bufc[r] = slsrc[...]
    bufr[c] = slsrc[...]
    rsbuf[r] = psrc[mine]
    art[nrr:, :] = tests[...] * scale

    pl.semaphore_wait(bar, nr - 1 + nc - 1)

    send_p(lambda to: psrc.at[to // 2], rsbuf.at[r], RS1)
    wait(rsbuf.at[pl.ds(0, nr - 1)], rsem.at[RS1])
    part = rsbuf[0]
    for k in range(1, nr):
        part = part + rsbuf[k]
    zsrc1[...] = part
    zbuf1[c] = part
    send_z(zsrc1, zbuf1.at[c], Z1)
    send_p(lambda to: slsrc, bufc.at[r], SLC)
    wait(zbuf1.at[pl.ds(0, nc - 1)], rsem.at[Z1])
    part = zbuf1[0]
    for k in range(1, nc):
        part = part + zbuf1[k]
    agsrc1[...] = part[0:cr, :]
    my_rows = pl.ds(pl.multiple_of(mine * cr, cr), cr)
    apiv[my_rows, :] = part[0:cr, :]
    trow = part[cr : cr + 1, :]
    send_p(lambda to: agsrc1, apiv.at[my_rows], AG1, step=2)
    send_z(slsrc, bufr.at[c], SLR)

    wait(bufc.at[pl.ds(0, nr - 1)], rsem.at[SLC])

    def pieces(buf, n, at):
        out = []
        for k in range(n):
            row = buf[4 * k, at : at + 1, :]
            for s in range(1, 4):
                row = row + buf[4 * k + s, at : at + 1, :]
            out.append(row)
        return out

    ohc = onehot_rows(jnp.concatenate(pieces(bufc, pcc, SUB), axis=1))
    y_c = jnp.concatenate(pieces(bufc, pcc, SUB + 1), axis=1)
    di_c = 1.0 / jnp.sum(ohc * noise_col, axis=0, keepdims=True)
    a_c = bufc[:, 0:SUB, :].reshape(ncc, LANES)
    hs_c = half_sq_row(a_c)
    ohp_t = onehot_rows(trow)
    t_col = row_to_col(jnp.broadcast_to(trow, (NP, NP)), eye)
    ohp = (iota((NP, TASKS), 1).astype(F32) == t_col).astype(F32)
    covp = mm(ohp, cov)

    n_ag = chunks - 1
    wait(apiv.at[pl.ds(0, n_ag * cr)], rsem.at[AG1])
    ap = apiv[...]
    hs_p = 0.5 * jnp.sum(ap * ap, axis=1, keepdims=True)

    def tile_p(a, hs, oh):
        return jnp.exp(mm_nt(ap, a) - hs_p - hs) * mm(covp, oh)

    pm = tile_p(ap, half_sq_row(ap), ohp_t)
    pmat[...] = pm
    nu = 1.0 / jnp.max(jnp.sum(jnp.abs(pm), axis=0, keepdims=True), axis=1, keepdims=True)
    eye_f = eye.astype(F32)
    fast = lax.Precision.DEFAULT
    w = (2.0 * eye_f - pm * nu) * nu
    for _ in range(3):
        w = mm(w, 2.0 * eye_f - mm(pm, w, fast), fast)
    w_t = w.T
    gtc = mm(w_t, tile_p(a_c, hs_c, ohc))
    gt_c[...] = gtc
    g_row = y_c * di_c
    left = jnp.concatenate([gt_c[my_rows, :] * di_c, jnp.broadcast_to(g_row, (8, ncc))], axis=0)
    bg = mm_nt(left, gtc)
    yy = jnp.sum(g_row * y_c, axis=1, keepdims=True)
    part = jnp.concatenate([bg[0 : cr + 1, :], jnp.broadcast_to(yy, (1, LANES))], axis=0)
    zsrc2[...] = part
    zbuf2[c] = part

    send_z(zsrc2, zbuf2.at[c], Z2)
    wait(bufr.at[pl.ds(0, nc - 1)], rsem.at[SLR])
    art[0:nrr, :] = bufr[:, 0:SUB, :].reshape(nrr, LANES)
    ohr = onehot_rows(jnp.concatenate(pieces(bufr, prr, SUB + 2), axis=1))
    y_r = jnp.concatenate(pieces(bufr, prr, SUB + 3), axis=1)
    d_r = jnp.sum(ohr * noise_col, axis=0, keepdims=True)
    di_r = 1.0 / d_r
    oht = onehot_rows(jnp.concatenate([ttasks[k : k + 1, :].astype(F32) for k in range(ntest)], axis=1))
    cov_rt = mm(cov, jnp.concatenate([ohr, oht], axis=1))
    a_rt = art[...]
    hs_rt = half_sq_row(a_rt)

    def k_chunk(k):
        a = bufc[4 * k : 4 * k + 4, 0:SUB, :].reshape(LANES, LANES)
        hs = 0.5 * jnp.sum(a * a, axis=1, keepdims=True)
        oh = jnp.transpose(ohc[:, k * LANES : (k + 1) * LANES])
        kmat[k * LANES : (k + 1) * LANES, :] = jnp.exp(mm_nt(a, a_rt) - hs - hs_rt) * mm(oh, cov_rt)

    for k in range(pcc):
        k_chunk(k)

    wait(zbuf2.at[pl.ds(0, nc - 1)], rsem.at[Z2])
    part = zbuf2[0]
    for k in range(1, nc):
        part = part + zbuf2[k]
    agsrc2[...] = part[0:cr, :]
    gram[my_rows, :] = part[0:cr, :]
    g = part[cr : cr + 1, :]
    yy = part[cr + 1 : cr + 2, :]
    send_p(lambda to: agsrc2, gram.at[my_rows], AG2, step=2)
    gt_r[...] = mm(w_t, tile_p(art[0:nrr, :], hs_rt[:, 0:nrr], ohr))
    a_own = inputs[...] * scale
    oho = onehot_rows(jnp.concatenate([tasks[k : k + 1, :].astype(F32) for k in range(nown)], axis=1))
    kp_own[...] = tile_p(a_own, half_sq_row(a_own), oho)
    base = mm(mm(w_t, pm), w)
    wait(gram.at[pl.ds(0, n_ag * cr)], rsem.at[AG2])
    mmat[...] = base + gram[...]

    def gj(_, carry):
        mmat[...] = eliminate(mmat[...], lane)
        pmat[...] = eliminate(pmat[...], lane)
        return carry

    lax.fori_loop(0, NP // 8, gj, 0)
    minv = mmat[...]
    x_col = jnp.sum(minv * g, axis=1, keepdims=True)
    x_row = diag_to_row(x_col, eye)
    gamma = yy[:, 0:1] - jnp.sum(g * x_row, axis=1, keepdims=True)
    rg = 1.0 / jnp.sqrt(gamma)
    q_c = (y_c - jnp.sum(gt_c[...] * x_col, axis=0, keepdims=True)) * di_c * rg
    q_r = (y_r - jnp.sum(gt_r[...] * x_col, axis=0, keepdims=True)) * di_r * rg
    q8 = jnp.concatenate(
        [q_c[:, k * LANES : (k + 1) * LANES] for k in range(pcc)] + [jnp.zeros((8 - pcc, LANES), F32)] * (pcc < 8), axis=0
    )
    qt = jnp.transpose(q8)
    acc = jnp.zeros((1, kmat.shape[1]), F32)
    for k in range(pcc):
        acc = acc + jnp.sum(kmat[k * LANES : (k + 1) * LANES, :] * qt[:, k : k + 1], axis=0, keepdims=True)
    for k in range(prr + ntest):
        zsrc3[k : k + 1, :] = acc[:, k * LANES : (k + 1) * LANES]

    send_z(zsrc3, zbuf3.at[c], Z3)
    zbuf3[c] = zsrc3[...]
    kp = kp_own[...]
    cov_d = jnp.sum(jnp.where(eye8, cov, 0.0), axis=1, keepdims=True)
    res = jnp.sum(oho * cov_d, axis=0, keepdims=True) - jnp.sum(mm(pmat[...], kp) * kp, axis=0, keepdims=True)
    for k in range(nown):
        res_o[k : k + 1, :] = res[:, k * LANES : (k + 1) * LANES]
    wait(zbuf3.at[pl.ds(0, nc - 1)], rsem.at[Z3])
    part = zbuf3[0]
    for k in range(1, nc):
        part = part + zbuf3[k]
    w_r = jnp.concatenate([part[k : k + 1, :] for k in range(prr)], axis=1) + d_r * q_r
    kq = part[prr:, :]
    gtr = gt_r[...]
    back = diag_to_row(jnp.sum(gtr * (w_r * di_r), axis=1, keepdims=True), eye)
    alpha = jnp.sum(w_r * q_r, axis=1, keepdims=True)
    part = jnp.concatenate([back, jnp.broadcast_to(alpha, (1, LANES))], axis=0)
    psrc3[...] = part
    pbuf3[r] = part
    send_p(lambda to: psrc3, pbuf3.at[r], P3)
    wait(pbuf3.at[pl.ds(0, nr - 1)], rsem.at[P3])
    part = pbuf3[0]
    for k in range(1, nr):
        part = part + pbuf3[k]
    alpha = part[1:2, 0:1]
    b_col = jnp.sum(minv * part[0:1, :], axis=1, keepdims=True)
    ln = (w_r - jnp.sum(gtr * b_col, axis=0, keepdims=True)) * di_r - alpha * q_r
    out = jnp.zeros((1, SUB), F32)
    for k in range(nc):
        out = out + jnp.where(c == k, ln[:, k * SUB : (k + 1) * SUB], 0.0)
    ln_o[...] = out
    tc_o[...] = kq * (1.0 / jnp.sqrt(alpha))

    wait(rsbuf.at[pl.ds(0, nr - 1)], ssem.at[RS1])
    wait(zbuf1.at[pl.ds(0, nc - 1)], ssem.at[Z1])
    wait(apiv.at[pl.ds(0, n_ag * cr)], ssem.at[AG1])
    wait(bufc.at[pl.ds(0, nr - 1)], ssem.at[SLC])
    wait(bufr.at[pl.ds(0, nc - 1)], ssem.at[SLR])
    wait(zbuf2.at[pl.ds(0, nc - 1)], ssem.at[Z2])
    wait(gram.at[pl.ds(0, n_ag * cr)], ssem.at[AG2])
    wait(zbuf3.at[pl.ds(0, nc - 1)], ssem.at[Z3])
    wait(pbuf3.at[pl.ds(0, nr - 1)], ssem.at[P3])


def per_device(
    nr, nc, inputs, tasks, targets, inv_length, task_factor, task_diag, noise, pivots, test_inputs, test_tasks
):
    rows_dev = inputs.shape[0]
    test_dev = test_inputs.shape[0]
    nown, ntest = rows_dev // LANES, test_dev // LANES
    chunks = nr // 2
    cr = NP // chunks
    nrr, ncc = nc * SUB, nr * SUB
    prr = nrr // LANES
    vmem = pl.BlockSpec(memory_space=pltpu.VMEM)
    smem = pl.BlockSpec(memory_space=pltpu.SMEM)

    def buf(*shape):
        return pltpu.VMEM(shape, F32)

    res, ln, tc = pl.pallas_call(
        functools.partial(kernel, nr, nc),
        out_shape=(
            jax.ShapeDtypeStruct((nown, LANES), F32),
            jax.ShapeDtypeStruct((1, SUB), F32),
            jax.ShapeDtypeStruct((ntest, LANES), F32),
        ),
        in_specs=[smem, smem] + [vmem] * 9,
        out_specs=(vmem, vmem, vmem),
        scratch_shapes=[
            buf(chunks, cr + 1, LANES), buf(nr, cr + 1, LANES), buf(cr + 1, LANES), buf(nc, cr + 1, LANES),
            buf(NP, LANES), buf(cr, LANES), buf(SUB + 4, LANES), buf(nr, SUB + 4, LANES), buf(nc, SUB + 4, LANES),
            buf(cr + 2, LANES), buf(nc, cr + 2, LANES), buf(cr, LANES), buf(NP, LANES),
            buf(prr + ntest, LANES), buf(nc, prr + ntest, LANES), buf(2, LANES), buf(nr, 2, LANES),
            buf(nrr + test_dev, LANES), buf(ncc, nrr + test_dev), buf(NP, ncc), buf(NP, nrr), buf(NP, rows_dev),
            buf(NP, NP), buf(NP, NP),
            pltpu.SemaphoreType.DMA((9,)), pltpu.SemaphoreType.DMA((9,)),
        ],
        compiler_params=pltpu.CompilerParams(
            collective_id=0, has_side_effects=True, vmem_limit_bytes=40 * 1024 * 1024
        ),
    )(
        pivots, tasks, inputs, tasks.reshape(nown, LANES), targets.reshape(nown, LANES), inv_length[None, :],
        task_factor, task_diag[None, :], noise[None, :], test_inputs, test_tasks.reshape(ntest, LANES),
    )
    return res.reshape(rows_dev), ln.reshape(SUB), tc.reshape(test_dev)


def solution(mesh):
    both = ("row", "col")
    return jax.shard_map(
        functools.partial(per_device, mesh.shape["row"], mesh.shape["col"]),
        mesh=mesh,
        in_specs=(P(both, None), P(both), P(both), P(), P(), P(), P(), P(), P("row", None), P("row")),
        out_specs=(P(both), P(both), P("row")),
        check_vma=False,
    )
```

```python
import functools

import jax
import jax.numpy as jnp
from jax import lax
from jax.experimental import pallas as pl
from jax.experimental.pallas import tpu as pltpu
from jax.sharding import PartitionSpec as P

TASKS = 8
PIV = 64
NP = 2 * PIV
SUB = 32
LANES = 128
HIGH = lax.Precision.HIGHEST
MESH = pl.DeviceIdType.MESH
F32 = jnp.float32

RS1, Z1, AG1, SLC, SIB, SLR, SLR2, Z2, AG2, Z3, P3 = range(11)
RADIX = 4


def iota(shape, axis):
    return lax.broadcasted_iota(jnp.int32, shape, axis)


def mm(a, b, precision=HIGH):
    return lax.dot_general(a, b, (((1,), (0,)), ((), ())), precision=precision, preferred_element_type=F32)


def mm_nt(a, b, precision=HIGH):
    return lax.dot_general(a, b, (((1,), (1,)), ((), ())), precision=precision, preferred_element_type=F32)


def diag_to_row(col, eye):
    return jnp.sum(jnp.where(eye, col, 0.0), axis=0, keepdims=True)


def row_to_col(row, eye):
    return jnp.sum(jnp.where(eye, row, 0.0), axis=1, keepdims=True)


def onehot_rows(task_row):
    n = task_row.shape[1]
    return (iota((TASKS, n), 0).astype(F32) == task_row).astype(F32)


def half_sq_row(a):
    ones = jnp.full((8, a.shape[1]), 0.5, F32)
    return mm_nt(ones, a * a)[0:1, :]


def eliminate(ref, b, lane):
    o = 8 * b
    inside = (lane >= o) & (lane < o + 8)
    top = ref[o : o + 8, :]
    cols = [jnp.broadcast_to(top[:, o + m : o + m + 1], (8, LANES)) for m in range(8)]
    d = [[cols[m][i : i + 1, :] for m in range(8)] for i in range(8)]
    rows = [jnp.where(inside, (lane == o + i).astype(F32), top[i : i + 1, :]) for i in range(8)]
    for m in range(8):
        inv = 1.0 / d[m][m]
        rows[m] = rows[m] * inv
        for j in range(m + 1, 8):
            d[m][j] = d[m][j] * inv
        for i in range(8):
            if i != m:
                f = d[i][m]
                rows[i] = rows[i] - f * rows[m]
                for j in range(m + 1, 8):
                    d[i][j] = d[i][j] - f * d[m][j]
    for t in range(1, NP // 8):
        k = 8 * ((b + t) % (NP // 8))
        body = ref[k : k + 8, :]
        acc = jnp.where(inside, 0.0, body)
        for m in range(8):
            acc = acc - body[:, o + m : o + m + 1] * rows[m]
        ref[k : k + 8, :] = acc
    ref[o : o + 8, :] = jnp.concatenate(rows, axis=0)


def eliminate_loop(ref, lane):
    def step(_, carry):
        for b in range(4):
            eliminate(ref, b, lane)
        x = pltpu.roll(ref[...], LANES - 32, axis=1)
        ref[...] = jnp.concatenate([x[32:], x[:32]], axis=0)
        return carry

    lax.fori_loop(0, NP // 32, step, 0)


def kernel(
    nr, nc,
    pivots_h, tasks_sh, inputs_h, tasks_h, targets_h, il_h, tfac_h, tdiag_h, noise_h, tests_h, ttasks_h,
    res_o, ln_o, tc_o,
    pivots, tasks_s, inputs, tasks, targets, il, tfac, tdiag, noise, tests, ttasks,
    psrc, rsbuf, zsrc1, zbuf1, apiv, agsrc1, slsrc, bufc, bufr,
    zsrc2, zbuf2, agsrc2, gram, zsrc3, zbuf3, psrc3, pbuf3,
    art, kmat, gt_c, gt_r, kp_own, mmat, pmat,
    ssem, rsem, lsem,
):
    r = lax.axis_index("row")
    c = lax.axis_index("col")
    me = r * nc + c
    chunks = nr // 2
    cr = NP // chunks
    mine = r // 2
    rows_dev = inputs.shape[0]
    nown = rows_dev // LANES
    ntest = tests.shape[0] // LANES
    nrr = nc * SUB
    ncc = nr * SUB
    prr, pcc = nrr // LANES, ncc // LANES

    def in_row(k):
        return lax.rem(r + k, nr)

    def in_col(k):
        return lax.rem(c + k, nc)

    loads = [
        pltpu.make_async_copy(src, dst, lsem.at[i])
        for i, (src, dst) in enumerate([
            (pivots_h, pivots), (tasks_sh, tasks_s), (inputs_h, inputs), (il_h, il), (tasks_h, tasks),
            (targets_h, targets), (tfac_h, tfac), (tdiag_h, tdiag), (noise_h, noise), (ttasks_h, ttasks),
            (tests_h, tests),
        ])
    ]
    for load in loads:
        load.start()

    order_z = sorted(range(1, nc), key=lambda k: -min(k, nc - k))
    order_p = list(range(1, nr))

    bar = pltpu.get_barrier_semaphore()
    for k in order_z:
        pl.semaphore_signal(bar, inc=1, device_id={"row": r, "col": in_col(k)}, device_id_type=MESH)
    for k in order_p:
        pl.semaphore_signal(bar, inc=1, device_id={"row": in_row(k), "col": c}, device_id_type=MESH)

    def send_z(src, dst, sem):
        for k in order_z:
            pltpu.make_async_remote_copy(
                src, dst, ssem.at[sem], rsem.at[sem], device_id={"row": r, "col": in_col(k)}, device_id_type=MESH
            ).start()

    def send_p(src_of, dst, sem, step=1):
        for k in order_p:
            if k % step == 0:
                to = in_row(k)
                pltpu.make_async_remote_copy(
                    src_of(to), dst, ssem.at[sem], rsem.at[sem], device_id={"row": to, "col": c}, device_id_type=MESH
                ).start()

    def send_one(src, dst, sem, dev):
        pltpu.make_async_remote_copy(
            src, dst, ssem.at[sem], rsem.at[sem], device_id=dev, device_id_type=MESH
        ).start()

    def wait(ref, sem):
        pltpu.make_async_copy(ref, ref, sem).wait()

    for load in loads:
        load.wait()
    lane = iota((1, LANES), 1)
    eye8 = iota((TASKS, TASKS), 0) == iota((TASKS, TASKS), 1)
    eye = iota((NP, NP), 0) == iota((NP, NP), 1)
    scale = il[...]
    cov = mm_nt(tfac[...], tfac[...]) + jnp.where(eye8, jnp.broadcast_to(tdiag[...], (TASKS, TASKS)), 0.0)
    noise_col = row_to_col(jnp.broadcast_to(noise[...], (TASKS, TASKS)), eye8)

    def pick(i, trow):
        piv = pivots[i // PIV, lax.rem(i, PIV)]
        own = (piv // rows_dev == me).astype(F32)
        loc = lax.rem(piv, rows_dev)
        row = inputs[pl.ds(loc, 1), :] * scale * own
        psrc[i // cr, pl.ds(lax.rem(i, cr), 1), :] = row
        return trow + jnp.where(lane == i, tasks_s[loc].astype(F32) * own, 0.0)

    trow = lax.fori_loop(0, NP, pick, jnp.zeros((1, LANES), F32))
    for j in range(chunks):
        psrc[j, cr : cr + 1, :] = trow

    slsrc[0:SUB, :] = inputs[0:SUB, :] * scale
    t_own = tasks[0:1, 0:SUB].astype(F32)
    y_own = targets[0:1, 0:SUB]
    t4 = jnp.concatenate([t_own] * 4, axis=1)
    y4 = jnp.concatenate([y_own] * 4, axis=1)
    core = lax.rem(r, 2)
    slot_r = core * chunks + mine
    groups = nc // RADIX
    turn = lax.rem(c, RADIX)
    slot_c = turn * groups + c // RADIX
    at_r = lane // SUB == lax.rem(slot_r, 4)
    at_c = lane // SUB == lax.rem(slot_c, 4)
    slsrc[SUB : SUB + 1, :] = jnp.where(at_r, t4, 0.0)
    slsrc[SUB + 1 : SUB + 2, :] = jnp.where(at_r, y4, 0.0)
    slsrc[SUB + 2 : SUB + 3, :] = jnp.where(at_c, t4, 0.0)
    slsrc[SUB + 3 : SUB + 4, :] = jnp.where(at_c, y4, 0.0)
    bufc[slot_r] = slsrc[...]
    bufr[slot_c] = slsrc[...]
    rsbuf[r] = psrc[mine]
    art[nrr:, :] = tests[...] * scale

    pl.semaphore_wait(bar, nr - 1 + nc - 1)

    send_p(lambda to: psrc.at[to // 2], rsbuf.at[r], RS1)
    for k in range(RADIX, nc, RADIX):
        send_one(slsrc, bufr.at[slot_c], SLR, {"row": r, "col": in_col(k)})
    wait(rsbuf.at[pl.ds(0, nr - 1)], rsem.at[RS1])
    part = rsbuf[0]
    for k in range(1, nr):
        part = part + rsbuf[k]
    zsrc1[...] = part
    zbuf1[c] = part
    send_z(zsrc1, zbuf1.at[c], Z1)
    send_p(lambda to: slsrc, bufc.at[slot_r], SLC, step=2)
    wait(zbuf1.at[pl.ds(0, nc - 1)], rsem.at[Z1])
    part = zbuf1[0]
    for k in range(1, nc):
        part = part + zbuf1[k]
    agsrc1[...] = part[0:cr, :]
    my_rows = pl.ds(pl.multiple_of(mine * cr, cr), cr)
    apiv[my_rows, :] = part[0:cr, :]
    trow = part[cr : cr + 1, :]
    send_p(lambda to: agsrc1, apiv.at[my_rows], AG1, step=2)
    wait(bufc.at[pl.ds(0, chunks - 1)], rsem.at[SLC])
    half = bufc.at[pl.ds(core * chunks, chunks)]
    send_one(half, half, SIB, {"row": r + 1 - 2 * core, "col": c})
    wait(bufr.at[pl.ds(0, groups - 1)], rsem.at[SLR])
    kin = bufr.at[pl.ds(turn * groups, groups)]
    for k in (1, nc - 1):
        send_one(kin, kin, SLR2, {"row": r, "col": in_col(k)})
    send_one(kin, kin, SLR2, {"row": r, "col": in_col(2 + (nc - 4) * lax.rem(c, 2))})

    wait(bufc.at[pl.ds(0, chunks)], rsem.at[SIB])

    def pieces(buf, n, at):
        out = []
        for k in range(n):
            row = buf[4 * k, at : at + 1, :]
            for s in range(1, 4):
                row = row + buf[4 * k + s, at : at + 1, :]
            out.append(row)
        return out

    ohc = onehot_rows(jnp.concatenate(pieces(bufc, pcc, SUB), axis=1))
    y_c = jnp.concatenate(pieces(bufc, pcc, SUB + 1), axis=1)
    di_c = 1.0 / jnp.sum(ohc * noise_col, axis=0, keepdims=True)
    a_c = bufc[:, 0:SUB, :].reshape(ncc, LANES)
    hs_c = half_sq_row(a_c)
    ohp_t = onehot_rows(trow)
    t_col = row_to_col(jnp.broadcast_to(trow, (NP, NP)), eye)
    ohp = (iota((NP, TASKS), 1).astype(F32) == t_col).astype(F32)
    covp = mm(ohp, cov)

    n_ag = chunks - 1
    wait(apiv.at[pl.ds(0, n_ag * cr)], rsem.at[AG1])
    ap = apiv[...]
    hs_p = 0.5 * jnp.sum(ap * ap, axis=1, keepdims=True)

    def tile_p(a, hs, oh):
        return jnp.exp(mm_nt(ap, a) - hs_p - hs) * mm(covp, oh)

    pm = tile_p(ap, half_sq_row(ap), ohp_t)
    pmat[...] = pm
    nu = 1.0 / jnp.max(jnp.sum(jnp.abs(pm), axis=0, keepdims=True), axis=1, keepdims=True)
    eye_f = eye.astype(F32)
    fast = lax.Precision.DEFAULT
    w = (2.0 * eye_f - pm * nu) * nu
    for _ in range(4):
        w = mm(w, 2.0 * eye_f - mm(pm, w, fast), fast)
    w_t = w.T
    gtc = mm(w_t, tile_p(a_c, hs_c, ohc))
    gt_c[...] = gtc
    g_row = y_c * di_c
    left = jnp.concatenate([gt_c[my_rows, :] * di_c, jnp.broadcast_to(g_row, (8, ncc))], axis=0)
    bg = mm_nt(left, gtc)
    yy = jnp.sum(g_row * y_c, axis=1, keepdims=True)
    part = jnp.concatenate([bg[0 : cr + 1, :], jnp.broadcast_to(yy, (1, LANES))], axis=0)
    zsrc2[...] = part
    zbuf2[c] = part

    send_z(zsrc2, zbuf2.at[c], Z2)
    oh_c = jnp.concatenate([jnp.transpose(ohc[:, k * LANES : (k + 1) * LANES]) for k in range(pcc)], axis=0)
    cov_c = mm(oh_c, cov)
    hs_cc = 0.5 * jnp.sum(a_c * a_c, axis=1, keepdims=True)

    def k_tile(at, a, oh):
        n = a.shape[0]
        kmat[:, at : at + n] = jnp.exp(mm_nt(a_c, a) - hs_cc - half_sq_row(a)) * mm(cov_c, oh)

    oht = onehot_rows(jnp.concatenate([ttasks[k : k + 1, :].astype(F32) for k in range(ntest)], axis=1))
    k_tile(nrr, art[nrr:, :], oht)
    wait(bufr.at[pl.ds(0, nc - groups)], rsem.at[SLR2])
    art[0:nrr, :] = bufr[:, 0:SUB, :].reshape(nrr, LANES)
    ohr = onehot_rows(jnp.concatenate(pieces(bufr, prr, SUB + 2), axis=1))
    y_r = jnp.concatenate(pieces(bufr, prr, SUB + 3), axis=1)
    d_r = jnp.sum(ohr * noise_col, axis=0, keepdims=True)
    di_r = 1.0 / d_r
    oht = onehot_rows(jnp.concatenate([ttasks[k : k + 1, :].astype(F32) for k in range(ntest)], axis=1))
    k_tile(0, art[0:nrr, :], ohr)

    wait(zbuf2.at[pl.ds(0, nc - 1)], rsem.at[Z2])
    part = zbuf2[0]
    for k in range(1, nc):
        part = part + zbuf2[k]
    agsrc2[...] = part[0:cr, :]
    gram[my_rows, :] = part[0:cr, :]
    g = part[cr : cr + 1, :]
    yy = part[cr + 1 : cr + 2, :]
    send_p(lambda to: agsrc2, gram.at[my_rows], AG2, step=2)
    a_r = art[0:nrr, :]
    gt_r[...] = mm(w_t, tile_p(a_r, half_sq_row(a_r), ohr))
    a_own = inputs[...] * scale
    oho = onehot_rows(jnp.concatenate([tasks[k : k + 1, :].astype(F32) for k in range(nown)], axis=1))
    kp_own[...] = tile_p(a_own, half_sq_row(a_own), oho)
    base = mm(mm(w_t, pm), w)
    wait(gram.at[pl.ds(0, n_ag * cr)], rsem.at[AG2])
    m0 = base + gram[...]
    mmat[...] = m0
    for b in range(NP // 8):
        eliminate(mmat, b, lane)
    minv = mmat[...]

    def solve(row):
        col = jnp.sum(minv * row, axis=1, keepdims=True)
        rest = row - jnp.sum(m0 * col, axis=0, keepdims=True)
        return col + jnp.sum(minv * rest, axis=1, keepdims=True)

    x_col = solve(g)
    x_row = diag_to_row(x_col, eye)
    gamma = yy[:, 0:1] - jnp.sum(g * x_row, axis=1, keepdims=True)
    rg = 1.0 / jnp.sqrt(gamma)
    q_c = (y_c - jnp.sum(gt_c[...] * x_col, axis=0, keepdims=True)) * di_c * rg
    q_r = (y_r - jnp.sum(gt_r[...] * x_col, axis=0, keepdims=True)) * di_r * rg
    q8 = jnp.concatenate(
        [q_c[:, k * LANES : (k + 1) * LANES] for k in range(pcc)] + [jnp.zeros((8 - pcc, LANES), F32)] * (pcc < 8), axis=0
    )
    qt = jnp.transpose(q8)
    acc = jnp.zeros((1, kmat.shape[1]), F32)
    for k in range(pcc):
        acc = acc + jnp.sum(kmat[k * LANES : (k + 1) * LANES, :] * qt[:, k : k + 1], axis=0, keepdims=True)
    for k in range(prr + ntest):
        zsrc3[k : k + 1, :] = acc[:, k * LANES : (k + 1) * LANES]

    send_z(zsrc3, zbuf3.at[c], Z3)
    zbuf3[c] = zsrc3[...]
    eliminate_loop(pmat, lane)
    kp = kp_own[...]
    cov_d = jnp.sum(jnp.where(eye8, cov, 0.0), axis=1, keepdims=True)
    res = jnp.sum(oho * cov_d, axis=0, keepdims=True) - jnp.sum(mm(pmat[...], kp) * kp, axis=0, keepdims=True)
    for k in range(nown):
        res_o[k : k + 1, :] = res[:, k * LANES : (k + 1) * LANES]
    wait(zbuf3.at[pl.ds(0, nc - 1)], rsem.at[Z3])
    part = zbuf3[0]
    for k in range(1, nc):
        part = part + zbuf3[k]
    w_r = jnp.concatenate([part[k : k + 1, :] for k in range(prr)], axis=1) + d_r * q_r
    kq = part[prr:, :]
    gtr = gt_r[...]
    back = diag_to_row(jnp.sum(gtr * (w_r * di_r), axis=1, keepdims=True), eye)
    alpha = jnp.sum(w_r * q_r, axis=1, keepdims=True)
    part = jnp.concatenate([back, jnp.broadcast_to(alpha, (1, LANES))], axis=0)
    psrc3[...] = part
    pbuf3[r] = part
    send_p(lambda to: psrc3, pbuf3.at[r], P3)
    wait(pbuf3.at[pl.ds(0, nr - 1)], rsem.at[P3])
    part = pbuf3[0]
    for k in range(1, nr):
        part = part + pbuf3[k]
    alpha = part[1:2, 0:1]
    b_col = solve(part[0:1, :])
    ln = (w_r - jnp.sum(gtr * b_col, axis=0, keepdims=True)) * di_r - alpha * q_r
    out = jnp.zeros((1, SUB), F32)
    for k in range(nc):
        out = out + jnp.where(slot_c == k, ln[:, k * SUB : (k + 1) * SUB], 0.0)
    ln_o[...] = out
    tc_o[...] = kq * (1.0 / jnp.sqrt(alpha))

    wait(rsbuf.at[pl.ds(0, nr - 1)], ssem.at[RS1])
    wait(zbuf1.at[pl.ds(0, nc - 1)], ssem.at[Z1])
    wait(apiv.at[pl.ds(0, n_ag * cr)], ssem.at[AG1])
    wait(bufc.at[pl.ds(0, chunks - 1)], ssem.at[SLC])
    wait(bufc.at[pl.ds(0, chunks)], ssem.at[SIB])
    wait(bufr.at[pl.ds(0, groups - 1)], ssem.at[SLR])
    wait(bufr.at[pl.ds(0, nc - groups)], ssem.at[SLR2])
    wait(zbuf2.at[pl.ds(0, nc - 1)], ssem.at[Z2])
    wait(gram.at[pl.ds(0, n_ag * cr)], ssem.at[AG2])
    wait(zbuf3.at[pl.ds(0, nc - 1)], ssem.at[Z3])
    wait(pbuf3.at[pl.ds(0, nr - 1)], ssem.at[P3])


def per_device(
    nr, nc, inputs, tasks, targets, inv_length, task_factor, task_diag, noise, pivots, test_inputs, test_tasks
):
    rows_dev = inputs.shape[0]
    test_dev = test_inputs.shape[0]
    nown, ntest = rows_dev // LANES, test_dev // LANES
    chunks = nr // 2
    cr = NP // chunks
    nrr, ncc = nc * SUB, nr * SUB
    prr = nrr // LANES
    vmem = pl.BlockSpec(memory_space=pltpu.VMEM)
    hbm = pl.BlockSpec(memory_space=pltpu.HBM)
    operands = (
        pivots, tasks, inputs, tasks.reshape(nown, LANES), targets.reshape(nown, LANES), inv_length[None, :],
        task_factor, task_diag[None, :], noise[None, :], test_inputs, test_tasks.reshape(ntest, LANES),
    )
    copies = [
        (pltpu.SMEM if i < 2 else pltpu.VMEM)(x.shape, x.dtype) for i, x in enumerate(operands)
    ]

    def buf(*shape):
        return pltpu.VMEM(shape, F32)

    res, ln, tc = pl.pallas_call(
        functools.partial(kernel, nr, nc),
        out_shape=(
            jax.ShapeDtypeStruct((nown, LANES), F32),
            jax.ShapeDtypeStruct((1, SUB), F32),
            jax.ShapeDtypeStruct((ntest, LANES), F32),
        ),
        in_specs=[hbm] * 11,
        out_specs=(vmem, vmem, vmem),
        scratch_shapes=copies + [
            buf(chunks, cr + 1, LANES), buf(nr, cr + 1, LANES), buf(cr + 1, LANES), buf(nc, cr + 1, LANES),
            buf(NP, LANES), buf(cr, LANES), buf(SUB + 4, LANES), buf(nr, SUB + 4, LANES), buf(nc, SUB + 4, LANES),
            buf(cr + 2, LANES), buf(nc, cr + 2, LANES), buf(cr, LANES), buf(NP, LANES),
            buf(prr + ntest, LANES), buf(nc, prr + ntest, LANES), buf(2, LANES), buf(nr, 2, LANES),
            buf(nrr + test_dev, LANES), buf(ncc, nrr + test_dev), buf(NP, ncc), buf(NP, nrr), buf(NP, rows_dev),
            buf(NP, NP), buf(NP, NP),
            pltpu.SemaphoreType.DMA((11,)), pltpu.SemaphoreType.DMA((11,)), pltpu.SemaphoreType.DMA((11,)),
        ],
        compiler_params=pltpu.CompilerParams(
            collective_id=0, has_side_effects=True, vmem_limit_bytes=62 * 1024 * 1024
        ),
    )(*operands)
    return res.reshape(rows_dev), ln.reshape(SUB), tc.reshape(test_dev)


def solution(mesh):
    both = ("row", "col")
    return jax.shard_map(
        functools.partial(per_device, mesh.shape["row"], mesh.shape["col"]),
        mesh=mesh,
        in_specs=(P(both, None), P(both), P(both), P(), P(), P(), P(), P(), P("row", None), P("row")),
        out_specs=(P(both), P(both), P("row")),
        check_vma=False,
    )
```

```python
import functools

import jax
import jax.numpy as jnp
from jax import lax
from jax.experimental import pallas as pl
from jax.experimental.pallas import tpu as pltpu
from jax.sharding import PartitionSpec as P

TASKS = 8
PIV = 64
NP = 2 * PIV
SUB = 32
LANES = 128
HIGH = lax.Precision.HIGHEST
MESH = pl.DeviceIdType.MESH
F32 = jnp.float32
BF16 = jnp.bfloat16

RS1, Z1, AG1, SLC, SIB, SLR, SLR2, Z2, AG2, Z3, P3 = range(11)
RADIX = 4


def iota(shape, axis):
    return lax.broadcasted_iota(jnp.int32, shape, axis)


def mm(a, b, precision=HIGH):
    return lax.dot_general(a, b, (((1,), (0,)), ((), ())), precision=precision, preferred_element_type=F32)


def mm_nt(a, b, precision=HIGH):
    return lax.dot_general(a, b, (((1,), (1,)), ((), ())), precision=precision, preferred_element_type=F32)


def split(a):
    high = a.astype(BF16).astype(F32)
    rest = a - high
    mid = rest.astype(BF16).astype(F32)
    return high, mid, rest - mid


def pack_left(a):
    high, mid, low = split(a)
    return jnp.concatenate([high, mid, high, mid, high, low], axis=1).astype(BF16)


def pack_right(a):
    high, mid, low = split(a)
    return jnp.concatenate([high, high, mid, mid, low, high], axis=1).astype(BF16)


def cross(left, right):
    return mm_nt(left, right, lax.Precision.DEFAULT)


def diag_to_row(col, eye):
    return jnp.sum(jnp.where(eye, col, 0.0), axis=0, keepdims=True)


def row_to_col(row, eye):
    return jnp.sum(jnp.where(eye, row, 0.0), axis=1, keepdims=True)


def onehot_rows(task_row):
    n = task_row.shape[1]
    return (iota((TASKS, n), 0).astype(F32) == task_row).astype(F32)


def half_sq_row(a):
    ones = jnp.full((8, a.shape[1]), 0.5, F32)
    return mm_nt(ones, a * a)[0:1, :]


def eliminate(ref, b, lane):
    o = 8 * b
    inside = (lane >= o) & (lane < o + 8)
    top = ref[o : o + 8, :]
    cols = [jnp.broadcast_to(top[:, o + m : o + m + 1], (8, LANES)) for m in range(8)]
    d = [[cols[m][i : i + 1, :] for m in range(8)] for i in range(8)]
    rows = [jnp.where(inside, (lane == o + i).astype(F32), top[i : i + 1, :]) for i in range(8)]
    for m in range(8):
        inv = 1.0 / d[m][m]
        rows[m] = rows[m] * inv
        for j in range(m + 1, 8):
            d[m][j] = d[m][j] * inv
        for i in range(8):
            if i != m:
                f = d[i][m]
                rows[i] = rows[i] - f * rows[m]
                for j in range(m + 1, 8):
                    d[i][j] = d[i][j] - f * d[m][j]
    for t in range(1, NP // 8):
        k = 8 * ((b + t) % (NP // 8))
        body = ref[k : k + 8, :]
        acc = jnp.where(inside, 0.0, body)
        for m in range(8):
            acc = acc - body[:, o + m : o + m + 1] * rows[m]
        ref[k : k + 8, :] = acc
    ref[o : o + 8, :] = jnp.concatenate(rows, axis=0)


def eliminate_loop(ref, lane):
    def step(_, carry):
        for b in range(4):
            eliminate(ref, b, lane)
        x = pltpu.roll(ref[...], LANES - 32, axis=1)
        ref[...] = jnp.concatenate([x[32:], x[:32]], axis=0)
        return carry

    lax.fori_loop(0, NP // 32, step, 0)


def kernel(
    nr, nc,
    pivots_h, tasks_sh, inputs_h, tasks_h, targets_h, il_h, tfac_h, tdiag_h, noise_h, tests_h, ttasks_h,
    res_o, ln_o, tc_o,
    pivots, tasks_s, inputs, tasks, targets, il, tfac, tdiag, noise, tests, ttasks,
    psrc, rsbuf, zsrc1, zbuf1, apiv, agsrc1, slsrc, bufc, bufr,
    zsrc2, zbuf2, agsrc2, gram, zsrc3, zbuf3, psrc3, pbuf3,
    art, kmat, gt_c, gt_r, kp_own, mmat, pmat,
    ssem, rsem, lsem,
):
    r = lax.axis_index("row")
    c = lax.axis_index("col")
    me = r * nc + c
    chunks = nr // 2
    cr = NP // chunks
    mine = r // 2
    rows_dev = inputs.shape[0]
    nown = rows_dev // LANES
    ntest = tests.shape[0] // LANES
    nrr = nc * SUB
    ncc = nr * SUB
    prr, pcc = nrr // LANES, ncc // LANES

    def in_row(k):
        return lax.rem(r + k, nr)

    def in_col(k):
        return lax.rem(c + k, nc)

    loads = [
        pltpu.make_async_copy(src, dst, lsem.at[i])
        for i, (src, dst) in enumerate([
            (pivots_h, pivots), (tasks_sh, tasks_s), (inputs_h, inputs), (il_h, il), (tasks_h, tasks),
            (targets_h, targets), (tfac_h, tfac), (tdiag_h, tdiag), (noise_h, noise), (ttasks_h, ttasks),
            (tests_h, tests),
        ])
    ]
    for load in loads:
        load.start()

    order_z = sorted(range(1, nc), key=lambda k: -min(k, nc - k))
    order_p = list(range(1, nr))

    bar = pltpu.get_barrier_semaphore()
    for k in order_z:
        pl.semaphore_signal(bar, inc=1, device_id={"row": r, "col": in_col(k)}, device_id_type=MESH)
    for k in order_p:
        pl.semaphore_signal(bar, inc=1, device_id={"row": in_row(k), "col": c}, device_id_type=MESH)

    def send_z(src, dst, sem):
        for k in order_z:
            pltpu.make_async_remote_copy(
                src, dst, ssem.at[sem], rsem.at[sem], device_id={"row": r, "col": in_col(k)}, device_id_type=MESH
            ).start()

    def send_p(src_of, dst, sem, step=1):
        for k in order_p:
            if k % step == 0:
                to = in_row(k)
                pltpu.make_async_remote_copy(
                    src_of(to), dst, ssem.at[sem], rsem.at[sem], device_id={"row": to, "col": c}, device_id_type=MESH
                ).start()

    def send_one(src, dst, sem, dev):
        pltpu.make_async_remote_copy(
            src, dst, ssem.at[sem], rsem.at[sem], device_id=dev, device_id_type=MESH
        ).start()

    def wait(ref, sem):
        pltpu.make_async_copy(ref, ref, sem).wait()

    for load in loads:
        load.wait()
    lane = iota((1, LANES), 1)
    eye8 = iota((TASKS, TASKS), 0) == iota((TASKS, TASKS), 1)
    eye = iota((NP, NP), 0) == iota((NP, NP), 1)
    scale = il[...]
    cov = mm_nt(tfac[...], tfac[...]) + jnp.where(eye8, jnp.broadcast_to(tdiag[...], (TASKS, TASKS)), 0.0)
    noise_col = row_to_col(jnp.broadcast_to(noise[...], (TASKS, TASKS)), eye8)

    def pick(i, trow):
        piv = pivots[i // PIV, lax.rem(i, PIV)]
        own = (piv // rows_dev == me).astype(F32)
        loc = lax.rem(piv, rows_dev)
        row = inputs[pl.ds(loc, 1), :] * scale * own
        psrc[i // cr, pl.ds(lax.rem(i, cr), 1), :] = row
        return trow + jnp.where(lane == i, tasks_s[loc].astype(F32) * own, 0.0)

    trow = lax.fori_loop(0, NP, pick, jnp.zeros((1, LANES), F32))
    for j in range(chunks):
        psrc[j, cr : cr + 1, :] = trow

    slsrc[0:SUB, :] = inputs[0:SUB, :] * scale
    t_own = tasks[0:1, 0:SUB].astype(F32)
    y_own = targets[0:1, 0:SUB]
    t4 = jnp.concatenate([t_own] * 4, axis=1)
    y4 = jnp.concatenate([y_own] * 4, axis=1)
    core = lax.rem(r, 2)
    slot_r = core * chunks + mine
    groups = nc // RADIX
    turn = lax.rem(c, RADIX)
    slot_c = turn * groups + c // RADIX
    at_r = lane // SUB == lax.rem(slot_r, 4)
    at_c = lane // SUB == lax.rem(slot_c, 4)
    slsrc[SUB : SUB + 1, :] = jnp.where(at_r, t4, 0.0)
    slsrc[SUB + 1 : SUB + 2, :] = jnp.where(at_r, y4, 0.0)
    slsrc[SUB + 2 : SUB + 3, :] = jnp.where(at_c, t4, 0.0)
    slsrc[SUB + 3 : SUB + 4, :] = jnp.where(at_c, y4, 0.0)
    bufc[slot_r] = slsrc[...]
    bufr[slot_c] = slsrc[...]
    rsbuf[r] = psrc[mine]
    art[nrr:, :] = tests[...] * scale

    pl.semaphore_wait(bar, nr - 1 + nc - 1)

    send_p(lambda to: psrc.at[to // 2], rsbuf.at[r], RS1)
    for k in range(RADIX, nc, RADIX):
        send_one(slsrc, bufr.at[slot_c], SLR, {"row": r, "col": in_col(k)})
    wait(rsbuf.at[pl.ds(0, nr - 1)], rsem.at[RS1])
    part = rsbuf[0]
    for k in range(1, nr):
        part = part + rsbuf[k]
    zsrc1[...] = part
    zbuf1[c] = part
    send_z(zsrc1, zbuf1.at[c], Z1)
    send_p(lambda to: slsrc, bufc.at[slot_r], SLC, step=2)
    wait(zbuf1.at[pl.ds(0, nc - 1)], rsem.at[Z1])
    part = zbuf1[0]
    for k in range(1, nc):
        part = part + zbuf1[k]
    agsrc1[...] = part[0:cr, :]
    my_rows = pl.ds(pl.multiple_of(mine * cr, cr), cr)
    apiv[my_rows, :] = part[0:cr, :]
    trow = part[cr : cr + 1, :]
    send_p(lambda to: agsrc1, apiv.at[my_rows], AG1, step=2)
    wait(bufc.at[pl.ds(0, chunks - 1)], rsem.at[SLC])
    half = bufc.at[pl.ds(core * chunks, chunks)]
    send_one(half, half, SIB, {"row": r + 1 - 2 * core, "col": c})
    wait(bufr.at[pl.ds(0, groups - 1)], rsem.at[SLR])
    kin = bufr.at[pl.ds(turn * groups, groups)]
    for k in (1, nc - 1):
        send_one(kin, kin, SLR2, {"row": r, "col": in_col(k)})
    send_one(kin, kin, SLR2, {"row": r, "col": in_col(2 + (nc - 4) * lax.rem(c, 2))})

    wait(bufc.at[pl.ds(0, chunks)], rsem.at[SIB])

    def pieces(buf, n, at):
        out = []
        for k in range(n):
            row = buf[4 * k, at : at + 1, :]
            for s in range(1, 4):
                row = row + buf[4 * k + s, at : at + 1, :]
            out.append(row)
        return out

    ohc = onehot_rows(jnp.concatenate(pieces(bufc, pcc, SUB), axis=1))
    y_c = jnp.concatenate(pieces(bufc, pcc, SUB + 1), axis=1)
    di_c = 1.0 / jnp.sum(ohc * noise_col, axis=0, keepdims=True)
    a_c = bufc[:, 0:SUB, :].reshape(ncc, LANES)
    hs_c = half_sq_row(a_c)
    left_c = pack_left(a_c)
    ohp_t = onehot_rows(trow)
    t_col = row_to_col(jnp.broadcast_to(trow, (NP, NP)), eye)
    ohp = (iota((NP, TASKS), 1).astype(F32) == t_col).astype(F32)
    covp = mm(ohp, cov)

    n_ag = chunks - 1
    wait(apiv.at[pl.ds(0, n_ag * cr)], rsem.at[AG1])
    ap = apiv[...]
    hs_p = 0.5 * jnp.sum(ap * ap, axis=1, keepdims=True)

    left_p = pack_left(ap)
    right_p = pack_right(ap)

    def tile_p(dots, hs, oh):
        return jnp.exp(dots - hs_p - hs) * mm(covp, oh)

    pm = tile_p(cross(left_p, right_p), half_sq_row(ap), ohp_t)
    pmat[...] = pm
    nu = 1.0 / jnp.max(jnp.sum(jnp.abs(pm), axis=0, keepdims=True), axis=1, keepdims=True)
    eye_f = eye.astype(F32)
    fast = lax.Precision.DEFAULT
    w = (2.0 * eye_f - pm * nu) * nu
    for _ in range(3):
        w = mm(w, 2.0 * eye_f - mm(pm, w, fast), fast)
    w_t = w.T
    gtc = mm(w_t, tile_p(cross(right_p, left_c), hs_c, ohc))
    gt_c[...] = gtc
    g_row = y_c * di_c
    left = jnp.concatenate([gt_c[my_rows, :] * di_c, jnp.broadcast_to(g_row, (8, ncc))], axis=0)
    bg = mm_nt(left, gtc)
    yy = jnp.sum(g_row * y_c, axis=1, keepdims=True)
    part = jnp.concatenate([bg[0 : cr + 1, :], jnp.broadcast_to(yy, (1, LANES))], axis=0)
    zsrc2[...] = part
    zbuf2[c] = part

    send_z(zsrc2, zbuf2.at[c], Z2)
    oh3 = jnp.concatenate([ohc] * 3, axis=0)
    oh_c = jnp.concatenate([jnp.transpose(oh3[:, k * LANES : (k + 1) * LANES]) for k in range(pcc)], axis=0).astype(BF16)
    hs_cc = 0.5 * jnp.sum(a_c * a_c, axis=1, keepdims=True)

    def k_tile(at, a, right, oh):
        n = a.shape[0]
        cov3 = jnp.concatenate(split(mm(cov, oh)), axis=0).astype(BF16)
        task = mm(oh_c, cov3, lax.Precision.DEFAULT)
        kmat[:, at : at + n] = jnp.exp(cross(left_c, right) - hs_cc - half_sq_row(a)) * task

    oht = onehot_rows(jnp.concatenate([ttasks[k : k + 1, :].astype(F32) for k in range(ntest)], axis=1))
    a_t = art[nrr:, :]
    k_tile(nrr, a_t, pack_right(a_t), oht)
    wait(bufr.at[pl.ds(0, nc - groups)], rsem.at[SLR2])
    art[0:nrr, :] = bufr[:, 0:SUB, :].reshape(nrr, LANES)
    ohr = onehot_rows(jnp.concatenate(pieces(bufr, prr, SUB + 2), axis=1))
    y_r = jnp.concatenate(pieces(bufr, prr, SUB + 3), axis=1)
    d_r = jnp.sum(ohr * noise_col, axis=0, keepdims=True)
    di_r = 1.0 / d_r
    oht = onehot_rows(jnp.concatenate([ttasks[k : k + 1, :].astype(F32) for k in range(ntest)], axis=1))
    a_r = art[0:nrr, :]
    right_r = pack_right(a_r)
    k_tile(0, a_r, right_r, ohr)

    wait(zbuf2.at[pl.ds(0, nc - 1)], rsem.at[Z2])
    part = zbuf2[0]
    for k in range(1, nc):
        part = part + zbuf2[k]
    agsrc2[...] = part[0:cr, :]
    gram[my_rows, :] = part[0:cr, :]
    g = part[cr : cr + 1, :]
    yy = part[cr + 1 : cr + 2, :]
    send_p(lambda to: agsrc2, gram.at[my_rows], AG2, step=2)
    gt_r[...] = mm(w_t, tile_p(cross(left_p, right_r), half_sq_row(a_r), ohr))
    a_own = inputs[...] * scale
    oho = onehot_rows(jnp.concatenate([tasks[k : k + 1, :].astype(F32) for k in range(nown)], axis=1))
    kp_own[...] = tile_p(cross(left_p, pack_right(a_own)), half_sq_row(a_own), oho)
    base = mm(mm(w_t, pm), w)
    wait(gram.at[pl.ds(0, n_ag * cr)], rsem.at[AG2])
    m0 = base + gram[...]
    mmat[...] = m0
    for b in range(NP // 8):
        eliminate(mmat, b, lane)
    minv = mmat[...]

    def solve(row):
        col = jnp.sum(minv * row, axis=1, keepdims=True)
        rest = row - jnp.sum(m0 * col, axis=0, keepdims=True)
        return col + jnp.sum(minv * rest, axis=1, keepdims=True)

    x_col = solve(g)
    x_row = diag_to_row(x_col, eye)
    gamma = yy[:, 0:1] - jnp.sum(g * x_row, axis=1, keepdims=True)
    rg = 1.0 / jnp.sqrt(gamma)
    q_c = (y_c - jnp.sum(gt_c[...] * x_col, axis=0, keepdims=True)) * di_c * rg
    q_r = (y_r - jnp.sum(gt_r[...] * x_col, axis=0, keepdims=True)) * di_r * rg
    q8 = jnp.concatenate(
        [q_c[:, k * LANES : (k + 1) * LANES] for k in range(pcc)] + [jnp.zeros((8 - pcc, LANES), F32)] * (pcc < 8), axis=0
    )
    qt = jnp.transpose(q8)
    acc = jnp.zeros((1, kmat.shape[1]), F32)
    for k in range(pcc):
        acc = acc + jnp.sum(kmat[k * LANES : (k + 1) * LANES, :] * qt[:, k : k + 1], axis=0, keepdims=True)
    for k in range(prr + ntest):
        zsrc3[k : k + 1, :] = acc[:, k * LANES : (k + 1) * LANES]

    send_z(zsrc3, zbuf3.at[c], Z3)
    zbuf3[c] = zsrc3[...]
    eliminate_loop(pmat, lane)
    kp = kp_own[...]
    cov_d = jnp.sum(jnp.where(eye8, cov, 0.0), axis=1, keepdims=True)
    res = jnp.sum(oho * cov_d, axis=0, keepdims=True) - jnp.sum(mm(pmat[...], kp) * kp, axis=0, keepdims=True)
    for k in range(nown):
        res_o[k : k + 1, :] = res[:, k * LANES : (k + 1) * LANES]
    wait(zbuf3.at[pl.ds(0, nc - 1)], rsem.at[Z3])
    part = zbuf3[0]
    for k in range(1, nc):
        part = part + zbuf3[k]
    w_r = jnp.concatenate([part[k : k + 1, :] for k in range(prr)], axis=1) + d_r * q_r
    kq = part[prr:, :]
    gtr = gt_r[...]
    back = diag_to_row(jnp.sum(gtr * (w_r * di_r), axis=1, keepdims=True), eye)
    alpha = jnp.sum(w_r * q_r, axis=1, keepdims=True)
    part = jnp.concatenate([back, jnp.broadcast_to(alpha, (1, LANES))], axis=0)
    psrc3[...] = part
    pbuf3[r] = part
    send_p(lambda to: psrc3, pbuf3.at[r], P3)
    wait(pbuf3.at[pl.ds(0, nr - 1)], rsem.at[P3])
    part = pbuf3[0]
    for k in range(1, nr):
        part = part + pbuf3[k]
    alpha = part[1:2, 0:1]
    b_col = jnp.sum(minv * part[0:1, :], axis=1, keepdims=True)
    ln = (w_r - jnp.sum(gtr * b_col, axis=0, keepdims=True)) * di_r - alpha * q_r
    out = jnp.zeros((1, SUB), F32)
    for k in range(nc):
        out = out + jnp.where(slot_c == k, ln[:, k * SUB : (k + 1) * SUB], 0.0)
    ln_o[...] = out
    tc_o[...] = kq * (1.0 / jnp.sqrt(alpha))

    wait(rsbuf.at[pl.ds(0, nr - 1)], ssem.at[RS1])
    wait(zbuf1.at[pl.ds(0, nc - 1)], ssem.at[Z1])
    wait(apiv.at[pl.ds(0, n_ag * cr)], ssem.at[AG1])
    wait(bufc.at[pl.ds(0, chunks - 1)], ssem.at[SLC])
    wait(bufc.at[pl.ds(0, chunks)], ssem.at[SIB])
    wait(bufr.at[pl.ds(0, groups - 1)], ssem.at[SLR])
    wait(bufr.at[pl.ds(0, nc - groups)], ssem.at[SLR2])
    wait(zbuf2.at[pl.ds(0, nc - 1)], ssem.at[Z2])
    wait(gram.at[pl.ds(0, n_ag * cr)], ssem.at[AG2])
    wait(zbuf3.at[pl.ds(0, nc - 1)], ssem.at[Z3])
    wait(pbuf3.at[pl.ds(0, nr - 1)], ssem.at[P3])


def hand_out(res_i, ln_i, tc_i, res_o, ln_o, tc_o, sem):
    moves = [
        pltpu.make_async_copy(src, dst, sem.at[i])
        for i, (src, dst) in enumerate([(res_i, res_o), (ln_i, ln_o), (tc_i, tc_o)])
    ]
    for move in moves:
        move.start()
    for move in moves:
        move.wait()


def per_device(
    nr, nc, inputs, tasks, targets, inv_length, task_factor, task_diag, noise, pivots, test_inputs, test_tasks
):
    rows_dev = inputs.shape[0]
    test_dev = test_inputs.shape[0]
    nown, ntest = rows_dev // LANES, test_dev // LANES
    chunks = nr // 2
    cr = NP // chunks
    nrr, ncc = nc * SUB, nr * SUB
    prr = nrr // LANES
    vmem = pl.BlockSpec(memory_space=pltpu.VMEM)
    hbm = pl.BlockSpec(memory_space=pltpu.HBM)
    operands = (
        pivots, tasks, inputs, tasks.reshape(nown, LANES), targets.reshape(nown, LANES), inv_length[None, :],
        task_factor, task_diag[None, :], noise[None, :], test_inputs, test_tasks.reshape(ntest, LANES),
    )
    copies = [
        (pltpu.SMEM if i < 2 else pltpu.VMEM)(x.shape, x.dtype) for i, x in enumerate(operands)
    ]

    def buf(*shape):
        return pltpu.VMEM(shape, F32)

    res, ln, tc = pl.pallas_call(
        functools.partial(kernel, nr, nc),
        out_shape=(
            jax.ShapeDtypeStruct((nown, LANES), F32),
            jax.ShapeDtypeStruct((1, SUB), F32),
            jax.ShapeDtypeStruct((ntest, LANES), F32),
        ),
        in_specs=[hbm] * 11,
        out_specs=(vmem, vmem, vmem),
        scratch_shapes=copies + [
            buf(chunks, cr + 1, LANES), buf(nr, cr + 1, LANES), buf(cr + 1, LANES), buf(nc, cr + 1, LANES),
            buf(NP, LANES), buf(cr, LANES), buf(SUB + 4, LANES), buf(nr, SUB + 4, LANES), buf(nc, SUB + 4, LANES),
            buf(cr + 2, LANES), buf(nc, cr + 2, LANES), buf(cr, LANES), buf(NP, LANES),
            buf(prr + ntest, LANES), buf(nc, prr + ntest, LANES), buf(2, LANES), buf(nr, 2, LANES),
            buf(nrr + test_dev, LANES), buf(ncc, nrr + test_dev), buf(NP, ncc), buf(NP, nrr), buf(NP, rows_dev),
            buf(NP, NP), buf(NP, NP),
            pltpu.SemaphoreType.DMA((11,)), pltpu.SemaphoreType.DMA((11,)), pltpu.SemaphoreType.DMA((11,)),
        ],
        compiler_params=pltpu.CompilerParams(
            collective_id=0, has_side_effects=True, vmem_limit_bytes=62 * 1024 * 1024
        ),
    )(*operands)
    res, ln, tc = pl.pallas_call(
        hand_out,
        out_shape=tuple(jax.ShapeDtypeStruct(x.shape, x.dtype) for x in (res, ln, tc)),
        in_specs=[hbm] * 3,
        out_specs=(hbm,) * 3,
        scratch_shapes=[pltpu.SemaphoreType.DMA((3,))],
        compiler_params=pltpu.CompilerParams(vmem_limit_bytes=62 * 1024 * 1024),
    )(res, ln, tc)
    return res.reshape(rows_dev), ln.reshape(SUB), tc.reshape(test_dev)


def solution(mesh):
    both = ("row", "col")
    return jax.shard_map(
        functools.partial(per_device, mesh.shape["row"], mesh.shape["col"]),
        mesh=mesh,
        in_specs=(P(both, None), P(both), P(both), P(), P(), P(), P(), P(), P("row", None), P("row")),
        out_specs=(P(both), P(both), P("row")),
        check_vma=False,
    )
```
